128 devices in a mesh: row: 8 (over x, y_lo), col: 16 (over y_hi, z, core).
Axes of the slice: x: 4, y: 4 (y_hi: 2, y_lo: 2; y = y_hi * 2 + y_lo), z: 4, core: 2. Of those that a mesh axis runs over, the one named last changes fastest.
Arguments:
- gradients: bfloat16 [3, 8, 256, 64, 128], P(None, 'row', 'col'), may hold values from -6 to 6
- tile_blocks: bfloat16 [49152, 128, 128], P(('row', 'col')), may hold values from -0.15625 to 0.15625
- tile_rows: int32 [49152], P(('row', 'col')), may hold values from 0 to 255
- tile_cols: int32 [49152], P(('row', 'col')), may hold values from 0 to 127
- tile_counts: int32 [128], P(('row', 'col')), may hold values from 48 to 384, as said below
Outputs:
- adjoint: bfloat16 [3, 16, 128, 64, 128], P(None, 'col', 'row')
The draws below stay inside these ranges and needn't reach their ends.
Inputs may be any that keep to these rules, and one draw needn't show every extreme that they name: `tile_counts`: some device uses all 384 slots; slots from a device's count on add nothing.
All inputs are finite; a program needn't handle non-finite values.
Results may differ from the reference program's by a relative error of at most 0.011.
Values may be sent and summed in bfloat16 or wider, within the bound.
A program may use at most 128 MiB of HBM per device.

```python
import jax
import jax.numpy as jnp
from jax import lax

BS = 128
NOBJ = 64
SETS = 3
SLOT_RATE = 24
TCAP = 384
BR = 256
BC = 128
SLOTS = 49152
N_ROW = 8
N_COL = 16
DEVICES = 128


def tile_layout(key):
    rows = jax.random.randint(jax.random.fold_in(key, 11), (DEVICES, TCAP), 0, BR)
    offsets = jax.random.randint(jax.random.fold_in(key, 12), (DEVICES, TCAP), -4, 5)
    device = jnp.arange(DEVICES, dtype=jnp.int32)[:, None]
    row_group = device // N_COL
    col_group = device % N_COL
    cols = jnp.mod(row_group * BR + rows - col_group * BC + offsets, BC)
    return (rows.reshape(-1).astype(jnp.int32), cols.reshape(-1).astype(jnp.int32))


def draw_tile_rows(key, part):
    rows, cols = tile_layout(key)
    return rows


def draw_tile_cols(key, part):
    rows, cols = tile_layout(key)
    return cols


def draw_tile_counts(key, part):
    key = jax.random.fold_in(key, 5)
    device = jnp.arange(DEVICES, dtype=jnp.int32)
    row_group = device // N_COL
    col_group = device % N_COL
    apart = jnp.abs((2 * col_group + 1) * N_ROW - (2 * row_group + 1) * N_COL) // (2 * N_ROW)
    level = TCAP // (1 + jnp.minimum(apart, 3))
    jitter = jax.random.randint(key, (DEVICES,), 0, level // 2 + 1)
    return jnp.where(apart == 0, TCAP, level - jitter).astype(jnp.int32)


def shard_levels(key, extent, split, smallest, top_value):
    level, own = 1.0, jax.random.fold_in(key, 6)
    for axis_at, blocks in split:
        draws = jnp.exp(jax.random.uniform(jax.random.fold_in(own, axis_at), (blocks,), jnp.float32, smallest / len(split), top_value / len(split)))
        level = level * jnp.repeat(draws, extent[axis_at] // blocks).reshape([-1 if axis == axis_at else 1 for axis in range(len(extent))])
    return level


def bell_draw(key, extent, width, bound, cuts=(), held_as=jnp.bfloat16):
    result = width * jax.random.normal(key, extent, jnp.float32)
    if cuts:
        result = result * shard_levels(key, extent, cuts, -0.22, 0.18)
    return jnp.clip(result, -bound, bound).astype(held_as)


def setup_inputs(seed: int = 0) -> dict:
    arg_keys = jax.random.split(jax.random.key(seed), 6)
    return {
        "gradients": bell_draw(arg_keys[0], (SETS, N_ROW, BR, NOBJ, BS), 1.0, 6.0, ((1, 8), (2, 16))),
        "tile_blocks": bell_draw(arg_keys[1], (SLOTS, BS, BS), (BS * SLOT_RATE // 2) ** -0.5, 0.15625, ((0, 128),)),
        "tile_rows": draw_tile_rows(jax.random.fold_in(arg_keys[5], 71), 0),
        "tile_cols": draw_tile_cols(jax.random.fold_in(arg_keys[5], 71), 0),
        "tile_counts": draw_tile_counts(jax.random.fold_in(arg_keys[5], 71), 0),
    }


def device_partial(row_panel, tile_data, row_ids, col_ids, live_count, column_blocks):
    slot_count = tile_data.shape[0]
    alive_mask = (jnp.arange(slot_count, dtype=jnp.int32) < live_count).astype(jnp.float32)
    picked = jnp.take(row_panel, row_ids, axis=1).astype(jnp.float32) * alive_mask[None, :, None, None]
    products_f = jnp.einsum("stjp,tpq->tsjq", picked, tile_data.astype(jnp.float32))
    summed = jax.ops.segment_sum(products_f, col_ids, num_segments=column_blocks)
    return jnp.transpose(summed, (1, 0, 2, 3))


def reference(gradients, tile_blocks, tile_rows, tile_cols, tile_counts):
    running = jnp.zeros((SETS, N_COL, BC, NOBJ, BS), jnp.float32)

    def advance(running, device):
        row_group = device // N_COL
        col_group = device % N_COL
        row_panel = lax.dynamic_index_in_dim(gradients, row_group, 1, keepdims=False)
        offset = (device * TCAP).astype(jnp.int32)
        tile_data = lax.dynamic_slice_in_dim(tile_blocks, offset, TCAP, 0)
        row_ids = lax.dynamic_slice_in_dim(tile_rows, offset, TCAP, 0)
        col_ids = lax.dynamic_slice_in_dim(tile_cols, offset, TCAP, 0)
        partial_value = device_partial(row_panel, tile_data, row_ids, col_ids, tile_counts[device], BC)
        current = lax.dynamic_index_in_dim(running, col_group, 1, keepdims=False)
        running = lax.dynamic_update_index_in_dim(running, current + partial_value, col_group, 1)
        return running, None

    running, unused = lax.scan(advance, running, jnp.arange(N_ROW * N_COL, dtype=jnp.int32))
    return running.astype(jnp.bfloat16)
```

```python
import functools

import jax
import jax.numpy as jnp
from jax import lax
from jax.experimental import pallas as pl
from jax.experimental.pallas import tpu as pltpu
from jax.sharding import PartitionSpec as P

MESH = pl.DeviceIdType.MESH
PARTS = 1
UNROLL = 32
BF16 = jnp.bfloat16
F32 = jnp.float32


def kernel(sets, row_ref, link_ref, grad_ref, tile_ref, out_ref, *scratch):
    units = sets * PARTS
    panels = scratch[:units]
    tiles, sums, partial, got_opp, got_far, got_pair, result, send_sem, recv_sem, own_sem, tile_sem, out_sem = scratch[units:]
    slots = tiles.shape[0]
    part = panels[0].shape[1]
    own_blocks = grad_ref.shape[2]

    row = lax.axis_index("row")
    col = lax.axis_index("col")
    x, y_lo = row // 2, row % 2
    y_hi, z, core = col // 8, (col // 2) % 4, col % 2

    def col_at(yh, zz, cc):
        return (yh * 4 + (zz + 4) % 4) * 2 + cc

    def row_at(xx, yl):
        return ((xx + 4) % 4) * 2 + yl

    z_up, z_down = (row, col_at(y_hi, z + 1, core)), (row, col_at(y_hi, z - 1, core))
    y_far, sibling = (row, col_at(1 - y_hi, z, core)), (row, col_at(y_hi, z, 1 - core))
    x_up, x_down = (row_at(x + 1, y_lo), col), (row_at(x - 1, y_lo), col)
    y_pair = (row_at(x, 1 - y_lo), col)

    barrier = pltpu.get_barrier_semaphore()
    for peer in (z_up, z_down, y_far, sibling, x_up, x_down, y_pair):
        pl.semaphore_signal(barrier, inc=1, device_id=peer, device_id_type=MESH)
    pl.semaphore_wait(barrier, 7)

    def remote(u, k, src, dst, peer):
        return pltpu.make_async_remote_copy(
            src_ref=src,
            dst_ref=dst,
            send_sem=send_sem.at[u, k],
            recv_sem=recv_sem.at[u, k],
            device_id=peer,
            device_id_type=MESH,
        )

    def own_slice(u):
        s, h = u // PARTS, u % PARTS
        return grad_ref.at[s, 0, :, pl.ds(h * part, part), :]

    def shard(u, yh, zz, first=0, count=own_blocks):
        return panels[u].at[pl.ds(col_at(yh, zz, core) * own_blocks + first, count)]

    half = own_blocks // 2
    other = 1 - y_hi

    def gather_copy(u, k):
        own = shard(u, y_hi, z)
        if k < 4:
            return remote(u, k, own_slice(u), own, (z_up, z_down, y_far, sibling)[k])
        src, peer = {
            4: (shard(u, other, z), z_up),
            5: (shard(u, other, z), z_down),
            6: (shard(u, y_hi, z - 1, 0, half), z_up),
            7: (shard(u, y_hi, z + 1, half, half), z_down),
            8: (shard(u, other, z - 1, 0, half), z_up),
            9: (shard(u, other, z + 1, half, half), z_down),
            10: (shard(u, other, z), sibling),
            11: (shard(u, y_hi, z - 1), sibling),
            12: (shard(u, y_hi, z + 1), sibling),
            13: (shard(u, other, z - 1), sibling),
            14: (shard(u, other, z + 1), sibling),
            15: (shard(u, y_hi, z + 2), sibling),
            16: (shard(u, other, z + 2), sibling),
        }[k]
        return remote(u, k, src, src, peer)

    def own_copy(u):
        return pltpu.make_async_copy(own_slice(u), shard(u, y_hi, z), own_sem.at[u])

    def send(u, *ks):
        for k in ks:
            gather_copy(u, k).start()

    def arrive(u, *ks):
        for k in ks:
            gather_copy(u, k).wait_recv()

    def own_y(u):
        send(u, 2)

    def own_z(u):
        send(u, 0, 1, 3)
        own_copy(u).start()

    def ring_own(u):
        arrive(u, 0)
        send(u, 6, 11)
        arrive(u, 1)
        send(u, 7, 12)

    def ring_other(u):
        arrive(u, 2)
        send(u, 4, 5, 10)

    def ring_other_half(u):
        arrive(u, 4)
        send(u, 8, 13)
        arrive(u, 5)
        send(u, 9, 14)

    def opposite_own(u):
        arrive(u, 6, 7)
        send(u, 15)

    def opposite_other(u):
        arrive(u, 8, 9)
        send(u, 16)

    def gathered(u):
        own_copy(u).wait()
        arrive(u, 3, 10, 11, 12, 13, 14, 15, 16)

    def products(u, first, count):
        def some(step, carry):
            for k in range(UNROLL):
                t = first + step * UNROLL + k
                picked = panels[u][row_ref[t]]
                sums[t] = sums[link_ref[t]] + jnp.dot(picked, tiles[t], preferred_element_type=F32)
            return carry

        lax.fori_loop(0, count // UNROLL, some, 0)

    def share(u, xx, yl):
        return partial.at[u, pl.ds(row_at(xx, yl) * own_blocks, own_blocks)]

    def collect(u, xx):
        first = row_at(xx, 0) * own_blocks

        def some(step, carry):
            for k in range(4):
                i = first + step * 4 + k
                partial[u, i] = sums[link_ref[slots + i]].astype(BF16)
            return carry

        lax.fori_loop(0, 2 * own_blocks // 4, some, 0)

    def reduce_copy(u, k):
        src, dst, peer = {
            17: (share(u, x + 2, 0), got_opp.at[u, 0], x_up),
            18: (share(u, x + 2, 1), got_opp.at[u, 1], x_down),
            19: (share(u, x + 1, 1), got_far.at[u, 0, 1], x_up),
            20: (share(u, x - 1, 0), got_far.at[u, 1, 0], x_down),
            21: (share(u, x + 1, 0), got_far.at[u, 0, 0], x_up),
            22: (share(u, x - 1, 1), got_far.at[u, 1, 1], x_down),
            23: (share(u, x, 1 - y_lo), got_pair.at[u], y_pair),
        }[k]
        return remote(u, k, src, dst, peer)

    def reduce_first(u):
        collect(u, x + 2)
        reduce_copy(u, 17).start()
        reduce_copy(u, 18).start()
        collect(u, x + 1)
        reduce_copy(u, 19).start()
        collect(u, x - 1)
        reduce_copy(u, 20).start()
        collect(u, x)

    def add_share(u, xx, yl, terms):
        first = row_at(xx, yl) * own_blocks

        def some(i, carry):
            total = partial[u, first + i].astype(F32)
            for term in terms:
                total = total + term(i).astype(F32)
            partial[u, first + i] = total.astype(BF16)
            return carry

        lax.fori_loop(0, own_blocks, some, 0)

    def reduce_second(u):
        reduce_copy(u, 17).wait_recv()
        add_share(u, x + 1, 0, [lambda i: got_opp[u, 0, i]])
        reduce_copy(u, 21).start()
        reduce_copy(u, 18).wait_recv()
        add_share(u, x - 1, 1, [lambda i: got_opp[u, 1, i]])
        reduce_copy(u, 22).start()

    def reduce_third(u):
        for k in (19, 20, 21, 22):
            reduce_copy(u, k).wait_recv()
        theirs = 1 - y_lo
        add_share(u, x, theirs, [lambda i: got_far[u, 0, theirs, i], lambda i: got_far[u, 1, theirs, i]])
        reduce_copy(u, 23).start()

    def out_copy(u):
        s, h = u // PARTS, u % PARTS
        return pltpu.make_async_copy(result.at[u], out_ref.at[s, 0, :, pl.ds(h * part, part), :], out_sem.at[u])

    def reduce_last(u):
        reduce_copy(u, 23).wait_recv()
        first = row_at(x, y_lo) * own_blocks

        def some(i, carry):
            total = partial[u, first + i].astype(F32) + got_far[u, 0, y_lo, i].astype(F32)
            total = total + got_far[u, 1, y_lo, i].astype(F32)
            result[u, i] = (total + got_pair[u, i].astype(F32)).astype(BF16)
            return carry

        lax.fori_loop(0, own_blocks, some, 0)
        out_copy(u).start()

    run = slots // 4
    tile_copies = [
        pltpu.make_async_copy(tile_ref.at[pl.ds(q * run, run)], tiles.at[pl.ds(q * run, run)], tile_sem.at[q])
        for q in range(4)
    ]
    own_y(0)
    own_z(0)
    for copy in tile_copies:
        copy.start()
    sums[slots] = jnp.zeros(sums.shape[1:], F32)

    def on(action, u):
        if 0 <= u < units:
            action(u)

    ring_own(0)
    on(own_z, 1)
    ring_other(0)
    on(own_y, 1)
    ring_other_half(0)
    opposite_own(0)
    opposite_other(0)
    gathered(0)
    for copy in tile_copies:
        copy.wait()
    for u in range(units):
        products(u, 0, run)
        on(ring_own, u + 1)
        on(own_z, u + 2)
        products(u, run, run)
        on(ring_other, u + 1)
        on(own_y, u + 2)
        products(u, 2 * run, run)
        on(reduce_third, u - 1)
        products(u, 3 * run, run)
        reduce_first(u)
        on(ring_other_half, u + 1)
        on(opposite_own, u + 1)
        on(reduce_second, u)
        on(reduce_last, u - 1)
        on(opposite_other, u + 1)
        on(gathered, u + 1)
    reduce_third(units - 1)
    reduce_last(units - 1)
    for u in range(units):
        for k in range(17):
            gather_copy(u, k).wait_send()
        for k in range(17, 24):
            reduce_copy(u, k).wait_send()
        out_copy(u).wait()


def shards(gradients, tile_blocks, tile_rows, tile_cols, tile_counts):
    sets, _, own_blocks, objectives, pores = gradients.shape
    slots = tile_blocks.shape[0]
    row_blocks = own_blocks * lax.axis_size("col")
    column_blocks = own_blocks * lax.axis_size("row")
    units, part = sets * PARTS, objectives // PARTS

    order = lax.iota(jnp.int32, slots)
    wanted = jnp.concatenate([tile_cols, lax.iota(jnp.int32, column_blocks)])
    limit = jnp.concatenate([order, jnp.broadcast_to(tile_counts, (column_blocks,))])
    match = (tile_cols[None, :] == wanted[:, None]) & (order[None, :] < limit[:, None])
    found = jnp.max(jnp.where(match, order[None, :], -1), axis=1)
    link = jnp.where(found < 0, slots, found)

    any_space = pl.BlockSpec(memory_space=pl.ANY)
    smem = pl.BlockSpec(memory_space=pltpu.SMEM)
    return pl.pallas_call(
        functools.partial(kernel, sets),
        out_shape=jax.ShapeDtypeStruct(gradients.shape, BF16),
        in_specs=[smem, smem, any_space, any_space],
        out_specs=any_space,
        scratch_shapes=[pltpu.VMEM((row_blocks, part, pores), BF16) for _ in range(units)]
        + [
            pltpu.VMEM((slots, pores, pores), BF16),
            pltpu.VMEM((slots + 1, part, pores), F32),
            pltpu.VMEM((units, column_blocks, part, pores), BF16),
            pltpu.VMEM((units, 2, own_blocks, part, pores), BF16),
            pltpu.VMEM((units, 2, 2, own_blocks, part, pores), BF16),
            pltpu.VMEM((units, own_blocks, part, pores), BF16),
            pltpu.VMEM((units, own_blocks, part, pores), BF16),
            pltpu.SemaphoreType.DMA((units, 24)),
            pltpu.SemaphoreType.DMA((units, 24)),
            pltpu.SemaphoreType.DMA((units,)),
            pltpu.SemaphoreType.DMA((4,)),
            pltpu.SemaphoreType.DMA((units,)),
        ],
        compiler_params=pltpu.CompilerParams(
            collective_id=0, has_side_effects=True, vmem_limit_bytes=60 * 2**20
        ),
        cost_estimate=pl.CostEstimate(
            flops=2 * sets * slots * objectives * pores * pores, bytes_accessed=slots * pores * pores * 2, transcendentals=0
        ),
    )(tile_rows, link, gradients, tile_blocks)


def solution(mesh):
    in_specs = (
        P(None, "row", "col", None, None),
        P(("row", "col"), None, None),
        P(("row", "col")),
        P(("row", "col")),
        P(("row", "col")),
    )
    out_specs = P(None, "col", "row", None, None)
    return jax.shard_map(shards, mesh=mesh, in_specs=in_specs, out_specs=out_specs, check_vma=False)
```

```python
import functools

import jax
import jax.numpy as jnp
from jax import lax
from jax.experimental import pallas as pl
from jax.experimental.pallas import tpu as pltpu
from jax.sharding import PartitionSpec as P

MESH = pl.DeviceIdType.MESH
PARTS = 2
SIDE = 4
ORDER = (
    ("own_z", 0), ("own_z", 2), ("own_z", 1), ("own_y", 3), ("own_y", 0), ("ring_other", 0), ("own_y", 1),
    ("ring_own_a", 0), ("ring_own_b", 0), ("own_y", 2), ("ring_other", 1), ("opposite_own", 0), ("half_b", 0),
    ("half_a", 0), ("own_y", 4), ("ring_own_b", 1), ("ring_own_a", 1), ("opposite_other", 0), ("own_z", 3),
    ("ring_other", 2), ("half_a", 1), ("half_b", 1), ("ring_own_a", 2), ("ring_own_b", 2), ("opposite_own", 1),
    ("gathered", 0), ("p0", 0), ("own_y", 5), ("p1", 0), ("p2", 0), ("opposite_other", 1), ("p3", 0),
    ("reduce_first", 0), ("gathered", 1), ("p0", 1), ("ring_other", 3), ("opposite_own", 2), ("p1", 1),
    ("half_a", 2), ("half_b", 2), ("p2", 1), ("p3", 1), ("reduce_first", 1), ("opposite_other", 2),
    ("ring_own_b", 3), ("own_z", 4), ("ring_own_a", 3), ("second_b", 0), ("gathered", 2), ("p0", 2), ("half_b", 3),
    ("second_a", 0), ("half_a", 3), ("p1", 2), ("ring_other", 4), ("opposite_own", 3), ("own_z", 5), ("p2", 2),
    ("p3", 2), ("opposite_other", 3), ("ring_other", 5), ("reduce_first", 2), ("gathered", 3), ("reduce_third", 0),
    ("p0", 3), ("ring_own_a", 4), ("second_a", 1), ("p1", 3), ("ring_own_b", 4), ("second_b", 1), ("p2", 3),
    ("p3", 3), ("ring_own_a", 5), ("half_b", 5), ("half_b", 4), ("opposite_own", 4), ("reduce_first", 3),
    ("half_a", 5), ("ring_own_b", 5), ("half_a", 4), ("opposite_other", 4), ("opposite_own", 5), ("gathered", 4),
    ("second_b", 2), ("second_a", 2), ("p0", 4), ("opposite_other", 5), ("p1", 4), ("second_a", 3), ("gathered", 5),
    ("second_b", 3), ("p2", 4), ("p3", 4), ("reduce_first", 4), ("reduce_third", 2), ("p0", 5), ("p1", 5),
    ("reduce_third", 3), ("p2", 5), ("p3", 5), ("reduce_first", 5), ("reduce_last", 2), ("reduce_last", 3),
    ("second_b", 4), ("reduce_third", 1), ("second_a", 4), ("second_a", 5), ("second_b", 5), ("reduce_third", 4),
    ("reduce_third", 5), ("reduce_last", 0), ("reduce_last", 1), ("reduce_last", 4), ("reduce_last", 5),
)
UNROLL = 32
LANES = 128
BF16 = jnp.bfloat16
F32 = jnp.float32


def kernel(sets, row_ref, col_ref, count_ref, cols_ref, grad_ref, tile_ref, out_ref, *scratch):
    units = sets * PARTS
    panels = scratch[:units]
    tiles, sums, partial, got_opp, got_far, got_pair, result, wanted, found, link_ref, send_sem, recv_sem, own_sem, tile_sem, out_sem, link_sem = scratch[units:]
    slots = tiles.shape[0]
    part = panels[0].shape[1]
    own_blocks = grad_ref.shape[2]

    row = lax.axis_index("row")
    col = lax.axis_index("col")
    x, y_lo = row // 2, row % 2
    y_hi, z, core = col // 8, (col // 2) % 4, col % 2

    def col_at(yh, zz, cc):
        return (yh * 4 + (zz + 4) % 4) * 2 + cc

    def row_at(xx, yl):
        return ((xx + 4) % 4) * 2 + yl

    z_up, z_down = (row, col_at(y_hi, z + 1, core)), (row, col_at(y_hi, z - 1, core))
    y_far, sibling = (row, col_at(1 - y_hi, z, core)), (row, col_at(y_hi, z, 1 - core))
    x_up, x_down = (row_at(x + 1, y_lo), col), (row_at(x - 1, y_lo), col)
    y_pair = (row_at(x, 1 - y_lo), col)

    barrier = pltpu.get_barrier_semaphore()
    for peer in (z_up, z_down, y_far, sibling, x_up, x_down, y_pair):
        pl.semaphore_signal(barrier, inc=1, device_id=peer, device_id_type=MESH)
    pl.semaphore_wait(barrier, 7)

    def remote(u, k, src, dst, peer):
        return pltpu.make_async_remote_copy(
            src_ref=src,
            dst_ref=dst,
            send_sem=send_sem.at[u, k],
            recv_sem=recv_sem.at[u, k],
            device_id=peer,
            device_id_type=MESH,
        )

    def own_slice(u):
        s, h = u // PARTS, u % PARTS
        return grad_ref.at[s, 0, :, pl.ds(h * part, part), :]

    def shard(u, yh, zz, first=0, count=own_blocks):
        return panels[u].at[pl.ds(col_at(yh, zz, core) * own_blocks + first, count)]

    half = own_blocks // 2
    other = 1 - y_hi

    def gather_copy(u, k):
        own = shard(u, y_hi, z)
        if k < 4:
            return remote(u, k, own_slice(u), own, (z_up, z_down, y_far, sibling)[k])
        src, peer = {
            4: (shard(u, other, z), z_up),
            5: (shard(u, other, z), z_down),
            6: (shard(u, y_hi, z - 1, 0, half), z_up),
            7: (shard(u, y_hi, z + 1, half, half), z_down),
            8: (shard(u, other, z - 1, 0, SIDE), z_up),
            9: (shard(u, other, z + 1, own_blocks - SIDE, SIDE), z_down),
            24: (shard(u, y_hi, z + 2, SIDE, own_blocks - 2 * SIDE), y_far),
            10: (shard(u, other, z), sibling),
            11: (shard(u, y_hi, z - 1), sibling),
            12: (shard(u, y_hi, z + 1), sibling),
            13: (shard(u, other, z - 1), sibling),
            14: (shard(u, other, z + 1), sibling),
            15: (shard(u, y_hi, z + 2), sibling),
            16: (shard(u, other, z + 2), sibling),
        }[k]
        return remote(u, k, src, src, peer)

    def own_copy(u):
        return pltpu.make_async_copy(own_slice(u), shard(u, y_hi, z), own_sem.at[u])

    def send(u, *ks):
        for k in ks:
            gather_copy(u, k).start()

    def arrive(u, *ks):
        for k in ks:
            gather_copy(u, k).wait_recv()

    def own_y(u):
        send(u, 2)

    def own_z(u):
        send(u, 0, 1, 3)
        own_copy(u).start()

    def ring_own_a(u):
        arrive(u, 0)
        send(u, 6, 11)

    def ring_own_b(u):
        arrive(u, 1)
        send(u, 7, 12)

    def ring_other(u):
        arrive(u, 2)
        send(u, 4, 5, 10)

    def half_a(u):
        arrive(u, 4)
        send(u, 8, 13)

    def half_b(u):
        arrive(u, 5)
        send(u, 9, 14)

    def opposite_own(u):
        arrive(u, 6, 7)
        send(u, 24, 15)

    def opposite_other(u):
        arrive(u, 8, 9, 24)
        send(u, 16)

    def gathered(u):
        own_copy(u).wait()
        arrive(u, 3, 10, 11, 12, 13, 14, 15, 16)

    def cols_copy(i):
        return pltpu.make_async_copy(cols_ref.at[pl.ds(i * LANES, LANES)], wanted.at[i], link_sem.at[i])

    def link_copy(i):
        return pltpu.make_async_copy(found.at[i], link_ref.at[pl.ds(i * LANES, LANES)], link_sem.at[i])

    def link_start():
        wanted[...] = jnp.zeros(wanted.shape, jnp.int32)
        for i in range(slots // LANES):
            cols_copy(i).start()

    def link_slots():
        for i in range(slots // LANES):
            cols_copy(i).wait()
        at = lax.broadcasted_iota(jnp.int32, wanted.shape, 0) * LANES + lax.broadcasted_iota(jnp.int32, wanted.shape, 1)
        target = jnp.where(at < slots, wanted[...], at - slots)
        limit = jnp.where(at < slots, at, count_ref[0])

        def some(step, latest):
            for k in range(16):
                t = step * 16 + k
                latest = jnp.where((target == col_ref[t]) & (limit > t), t, latest)
            return latest

        found[...] = lax.fori_loop(0, slots // 16, some, jnp.full(wanted.shape, slots, jnp.int32))
        for i in range(wanted.shape[0]):
            link_copy(i).start()
        for i in range(wanted.shape[0]):
            link_copy(i).wait()

    def products(u, first, count):
        def some(step, carry):
            for k in range(UNROLL):
                t = first + step * UNROLL + k
                picked = panels[u][row_ref[t]]
                sums[t] = sums[link_ref[t]] + jnp.dot(picked, tiles[t], preferred_element_type=F32)
            return carry

        lax.fori_loop(0, count // UNROLL, some, 0)

    def share(u, xx, yl):
        return partial.at[u, pl.ds(row_at(xx, yl) * own_blocks, own_blocks)]

    def collect(u, xx):
        first = row_at(xx, 0) * own_blocks

        def some(step, carry):
            for k in range(4):
                i = first + step * 4 + k
                partial[u, i] = sums[link_ref[slots + i]].astype(BF16)
            return carry

        lax.fori_loop(0, 2 * own_blocks // 4, some, 0)

    def reduce_copy(u, k):
        src, dst, peer = {
            17: (share(u, x + 2, 0), got_opp.at[u, 0], x_up),
            18: (share(u, x + 2, 1), got_opp.at[u, 1], x_down),
            19: (share(u, x + 1, 1), got_far.at[u, 0, 1], x_up),
            20: (share(u, x - 1, 0), got_far.at[u, 1, 0], x_down),
            21: (share(u, x + 1, 0), got_far.at[u, 0, 0], x_up),
            22: (share(u, x - 1, 1), got_far.at[u, 1, 1], x_down),
            23: (share(u, x, 1 - y_lo), got_pair.at[u], y_pair),
        }[k]
        return remote(u, k, src, dst, peer)

    def reduce_first(u):
        collect(u, x + 2)
        reduce_copy(u, 17).start()
        reduce_copy(u, 18).start()
        collect(u, x + 1)
        reduce_copy(u, 19).start()
        collect(u, x - 1)
        reduce_copy(u, 20).start()
        collect(u, x)

    def add_share(u, xx, yl, terms):
        first = row_at(xx, yl) * own_blocks

        def some(i, carry):
            total = partial[u, first + i].astype(F32)
            for term in terms:
                total = total + term(i).astype(F32)
            partial[u, first + i] = total.astype(BF16)
            return carry

        lax.fori_loop(0, own_blocks, some, 0)

    def second_a(u):
        reduce_copy(u, 17).wait_recv()
        add_share(u, x + 1, 0, [lambda i: got_opp[u, 0, i]])
        reduce_copy(u, 21).start()

    def second_b(u):
        reduce_copy(u, 18).wait_recv()
        add_share(u, x - 1, 1, [lambda i: got_opp[u, 1, i]])
        reduce_copy(u, 22).start()

    def reduce_third(u):
        for k in (19, 20, 21, 22):
            reduce_copy(u, k).wait_recv()
        theirs = 1 - y_lo
        add_share(u, x, theirs, [lambda i: got_far[u, 0, theirs, i], lambda i: got_far[u, 1, theirs, i]])
        reduce_copy(u, 23).start()

    def out_copy(u):
        s, h = u // PARTS, u % PARTS
        return pltpu.make_async_copy(result.at[u], out_ref.at[s, 0, :, pl.ds(h * part, part), :], out_sem.at[u])

    def reduce_last(u):
        reduce_copy(u, 23).wait_recv()
        first = row_at(x, y_lo) * own_blocks

        def some(i, carry):
            total = partial[u, first + i].astype(F32) + got_far[u, 0, y_lo, i].astype(F32)
            total = total + got_far[u, 1, y_lo, i].astype(F32)
            result[u, i] = (total + got_pair[u, i].astype(F32)).astype(BF16)
            return carry

        lax.fori_loop(0, own_blocks, some, 0)
        out_copy(u).start()

    run = slots // 4
    tile_copies = [
        pltpu.make_async_copy(tile_ref.at[pl.ds(q * run, run)], tiles.at[pl.ds(q * run, run)], tile_sem.at[q])
        for q in range(4)
    ]

    def product_run(q):
        def action(u):
            if u == 0:
                if q == 0:
                    link_slots()
                tile_copies[q].wait()
            products(u, q * run, run)

        return action

    actions = {f"p{q}": product_run(q) for q in range(4)}
    for action in (
        own_y, own_z, ring_own_a, ring_own_b, ring_other, half_a, half_b, opposite_own, opposite_other, gathered,
        reduce_first, second_a, second_b, reduce_third, reduce_last,
    ):
        actions[action.__name__] = action

    started = False
    for name, u in ORDER:
        if not started and name.startswith("ring"):
            started = True
            link_start()
            for copy in tile_copies:
                copy.start()
            sums[slots] = jnp.zeros(sums.shape[1:], F32)
        actions[name](u)
    for u in range(units):
        for k in (*range(17), 24):
            gather_copy(u, k).wait_send()
        for k in range(17, 24):
            reduce_copy(u, k).wait_send()
        out_copy(u).wait()


def shards(gradients, tile_blocks, tile_rows, tile_cols, tile_counts):
    sets, _, own_blocks, objectives, pores = gradients.shape
    slots = tile_blocks.shape[0]
    row_blocks = own_blocks * lax.axis_size("col")
    column_blocks = own_blocks * lax.axis_size("row")
    units, part = sets * PARTS, objectives // PARTS

    any_space = pl.BlockSpec(memory_space=pl.ANY)
    smem = pl.BlockSpec(memory_space=pltpu.SMEM)
    return pl.pallas_call(
        functools.partial(kernel, sets),
        out_shape=jax.ShapeDtypeStruct(gradients.shape, BF16),
        in_specs=[smem, smem, smem, any_space, any_space, any_space],
        out_specs=any_space,
        scratch_shapes=[pltpu.VMEM((row_blocks, part, pores), BF16) for _ in range(units)]
        + [
            pltpu.VMEM((slots, pores, pores), BF16),
            pltpu.VMEM((slots + 1, part, pores), F32),
            pltpu.VMEM((units, column_blocks, part, pores), BF16),
            pltpu.VMEM((units, 2, own_blocks, part, pores), BF16),
            pltpu.VMEM((units, 2, 2, own_blocks, part, pores), BF16),
            pltpu.VMEM((units, own_blocks, part, pores), BF16),
            pltpu.VMEM((units, own_blocks, part, pores), BF16),
            pltpu.VMEM(((slots + column_blocks) // LANES, LANES), jnp.int32),
            pltpu.VMEM(((slots + column_blocks) // LANES, LANES), jnp.int32),
            pltpu.SMEM((slots + column_blocks,), jnp.int32),
            pltpu.SemaphoreType.DMA((units, 25)),
            pltpu.SemaphoreType.DMA((units, 25)),
            pltpu.SemaphoreType.DMA((units,)),
            pltpu.SemaphoreType.DMA((4,)),
            pltpu.SemaphoreType.DMA((units,)),
            pltpu.SemaphoreType.DMA(((slots + column_blocks) // LANES,)),
        ],
        compiler_params=pltpu.CompilerParams(
            collective_id=0, has_side_effects=True, vmem_limit_bytes=60 * 2**20
        ),
        cost_estimate=pl.CostEstimate(
            flops=2 * sets * slots * objectives * pores * pores, bytes_accessed=slots * pores * pores * 2, transcendentals=0
        ),
    )(tile_rows, tile_cols, tile_counts, tile_cols, gradients, tile_blocks)


def solution(mesh):
    in_specs = (
        P(None, "row", "col", None, None),
        P(("row", "col"), None, None),
        P(("row", "col")),
        P(("row", "col")),
        P(("row", "col")),
    )
    out_specs = P(None, "col", "row", None, None)
    return jax.shard_map(shards, mesh=mesh, in_specs=in_specs, out_specs=out_specs, check_vma=False)
```

```python
import functools

import jax
import jax.numpy as jnp
from jax import lax
from jax.experimental import pallas as pl
from jax.experimental.pallas import tpu as pltpu
from jax.sharding import PartitionSpec as P

MESH = pl.DeviceIdType.MESH
PARTS = 2
SIDE = (4, 4, 4, 4, 4, 4)
PAIRED = (False, False, True, True, True, True)
ORDER = (
    ("own_z", 1), ("own_y", 1), ("own_z", 2), ("ring_other", 1), ("own_y", 0), ("own_y", 2), ("ring_own_b", 1),
    ("ring_own_a", 1), ("ring_own_b", 2), ("ring_own_a", 2), ("ring_other", 2), ("half_b", 1), ("half_a", 1),
    ("opposite_own", 1), ("opposite_other", 1), ("own_z", 0), ("own_y", 4), ("opposite_own", 2), ("own_y", 3),
    ("half_a", 2), ("half_b", 2), ("gathered", 1), ("p0", 1), ("ring_other", 0), ("p1", 1), ("p2", 1), ("own_z", 3),
    ("own_y", 5), ("ring_own_a", 0), ("ring_own_b", 0), ("opposite_other", 2), ("p3", 1), ("reduce_first", 1),
    ("gathered", 2), ("p0", 2), ("p1", 2), ("half_b", 0), ("half_a", 0), ("opposite_own", 0), ("ring_other", 3),
    ("p2", 2), ("ring_own_a", 3), ("p3", 2), ("opposite_other", 0), ("ring_own_b", 3), ("reduce_first", 2),
    ("own_z", 4), ("second_a", 1), ("second_b", 1), ("gathered", 0), ("p0", 0), ("half_b", 3), ("p1", 0),
    ("opposite_own", 3), ("half_a", 3), ("ring_other", 4), ("side", 2), ("p2", 0), ("p3", 0), ("opposite_other", 3),
    ("ring_own_b", 4), ("ring_own_a", 4), ("reduce_first", 0), ("own_z", 5), ("reduce_third", 1), ("gathered", 3),
    ("p0", 3), ("second_b", 2), ("p1", 3), ("half_a", 4), ("opposite_own", 4), ("half_b", 4), ("second_a", 2),
    ("ring_other", 5), ("p2", 3), ("p3", 3), ("opposite_other", 4), ("ring_own_a", 5), ("ring_own_b", 5),
    ("reduce_first", 3), ("second_b", 0), ("second_a", 0), ("gathered", 4), ("p0", 4), ("half_b", 5), ("half_a", 5),
    ("opposite_own", 5), ("p1", 4), ("p2", 4), ("side", 3), ("opposite_other", 5), ("p3", 4), ("reduce_first", 4),
    ("gathered", 5), ("p0", 5), ("reduce_third", 2), ("second_b", 3), ("second_a", 3), ("p1", 5), ("p2", 5),
    ("side", 4), ("p3", 5), ("reduce_first", 5), ("second_a", 4), ("reduce_third", 3), ("second_b", 4),
    ("reduce_third", 0), ("side", 5), ("second_b", 5), ("second_a", 5), ("reduce_third", 4), ("reduce_last", 0),
    ("reduce_last", 1), ("reduce_last", 2), ("reduce_third", 5), ("reduce_last", 4), ("reduce_last", 3),
    ("reduce_last", 5),
)
UNROLL = 32
LANES = 128
RECV = (0, 1, 2, 3, 4, 5, 6, 6, 7, 7, 3, 3, 3, 3, 3, 3, 3, 8, 9, 10, 10, 10, 10, 11, 7, 12)
ARRIVALS = 13
BF16 = jnp.bfloat16
F32 = jnp.float32


def kernel(sets, count_ref, rows_ref, cols_ref, grad_ref, tile_ref, out_ref, *scratch):
    units = sets * PARTS
    panels = scratch[:units]
    (
        tiles, sums, partial, got_opp, got_far, got_pair, got_side, result, wanted, found, link_ref, col_ref,
        send_sem, recv_sem, own_sem, tile_sem, out_sem, link_sem,
    ) = scratch[units:]
    slots = tiles.shape[0]
    part, pores = panels[0].shape[1:]
    own_blocks = grad_ref.shape[2]

    row = lax.axis_index("row")
    col = lax.axis_index("col")
    x, y_lo = row // 2, row % 2
    y_hi, z, core = col // 8, (col // 2) % 4, col % 2

    def col_at(yh, zz, cc):
        return (yh * 4 + (zz + 4) % 4) * 2 + cc

    def row_at(xx, yl):
        return ((xx + 4) % 4) * 2 + yl

    z_up, z_down = (row, col_at(y_hi, z + 1, core)), (row, col_at(y_hi, z - 1, core))
    y_far, sibling = (row, col_at(1 - y_hi, z, core)), (row, col_at(y_hi, z, 1 - core))
    x_up, x_down = (row_at(x + 1, y_lo), col), (row_at(x - 1, y_lo), col)
    y_pair = (row_at(x, 1 - y_lo), col)

    barrier = pltpu.get_barrier_semaphore()
    for peer in (z_up, z_down, y_far, sibling, x_up, x_down, y_pair):
        pl.semaphore_signal(barrier, inc=1, device_id=peer, device_id_type=MESH)
    pl.semaphore_wait(barrier, 7)

    def remote(u, k, src, dst, peer):
        return pltpu.make_async_remote_copy(
            src_ref=src,
            dst_ref=dst,
            send_sem=send_sem.at[u],
            recv_sem=recv_sem.at[u, RECV[k]],
            device_id=peer,
            device_id_type=MESH,
        )

    def landed(u, k, region):
        remote(u, k, region, region, sibling).wait_recv()

    def own_slice(u):
        s, h = u // PARTS, u % PARTS
        return grad_ref.at[s, 0, :, pl.ds(h * part, part), :]

    def shard(u, yh, zz, first=0, count=own_blocks):
        return panels[u].at[pl.ds((core * 8 + yh * 4 + (zz + 4) % 4) * own_blocks + first, count)]

    half = own_blocks // 2
    other = 1 - y_hi

    def gather_copy(u, k):
        own = shard(u, y_hi, z)
        if k < 4:
            return remote(u, k, own_slice(u), own, (z_up, z_down, y_far, sibling)[k])
        src, peer = {
            4: (shard(u, other, z), z_up),
            5: (shard(u, other, z), z_down),
            6: (shard(u, y_hi, z - 1, 0, half), z_up),
            7: (shard(u, y_hi, z + 1, half, half), z_down),
            8: (shard(u, other, z - 1, 0, SIDE[u]), z_up),
            9: (shard(u, other, z + 1, own_blocks - SIDE[u], SIDE[u]), z_down),
            24: (shard(u, y_hi, z + 2, SIDE[u], own_blocks - 2 * SIDE[u]), y_far),
            10: (shard(u, other, z), sibling),
            11: (shard(u, y_hi, z - 1), sibling),
            12: (shard(u, y_hi, z + 1), sibling),
            13: (shard(u, other, z - 1), sibling),
            14: (shard(u, other, z + 1), sibling),
            15: (shard(u, y_hi, z + 2), sibling),
            16: (shard(u, other, z + 2), sibling),
        }[k]
        return remote(u, k, src, src, peer)

    def own_copy(u):
        return pltpu.make_async_copy(own_slice(u), shard(u, y_hi, z), own_sem.at[u])

    def send(u, *ks):
        for k in ks:
            gather_copy(u, k).start()

    def arrive(u, *ks):
        for k in ks:
            gather_copy(u, k).wait_recv()

    def own_y(u):
        send(u, 2)

    def own_z(u):
        send(u, 0, 1, 3)
        own_copy(u).start()

    def ring_own_a(u):
        arrive(u, 0)
        send(u, 6, 11)

    def ring_own_b(u):
        arrive(u, 1)
        send(u, 7, 12)

    def ring_other(u):
        arrive(u, 2)
        send(u, 4, 5, 10)

    def half_a(u):
        arrive(u, 4)
        send(u, 8, 13)

    def half_b(u):
        arrive(u, 5)
        send(u, 9, 14)

    def opposite_own(u):
        landed(u, 6, shard(u, y_hi, z + 2))
        if SIDE[u] < half:
            send(u, 24)
        send(u, 15)

    def opposite_other(u):
        landed(u, 8, shard(u, other, z + 2))
        send(u, 16)

    def gathered(u):
        own_copy(u).wait()
        landed(u, 3, panels[u].at[pl.ds((1 - core) * 8 * own_blocks, 8 * own_blocks)])

    lines = slots // LANES
    linked = slots + partial.shape[1]
    link_lines = linked // LANES

    def index_copies():
        copies = [pltpu.make_async_copy(cols_ref, col_ref, link_sem.at[0])]
        for i in range(lines):
            run_i = pl.ds(i * LANES, LANES)
            copies.append(pltpu.make_async_copy(cols_ref.at[run_i], wanted.at[i], link_sem.at[1 + i]))
            copies.append(pltpu.make_async_copy(rows_ref.at[run_i], wanted.at[link_lines + i], link_sem.at[1 + lines + i]))
        return copies

    def link_start():
        wanted[...] = jnp.zeros(wanted.shape, jnp.int32)
        for copy in index_copies():
            copy.start()

    def link_slots():
        for copy in index_copies():
            copy.wait()
        shape = (link_lines, LANES)
        at = lax.broadcasted_iota(jnp.int32, shape, 0) * LANES + lax.broadcasted_iota(jnp.int32, shape, 1)
        target = jnp.where(at < slots, wanted[:link_lines], at - slots)
        limit = jnp.where(at < slots, at, count_ref[0])

        def some(step, latest):
            for k in range(16):
                t = step * 16 + k
                latest = jnp.where((target == col_ref[t]) & (limit > t), t, latest)
            return latest

        found[:link_lines] = lax.fori_loop(0, slots // 16, some, jnp.full(shape, slots, jnp.int32))
        rows = wanted[link_lines:]
        group = rows // own_blocks
        found[link_lines:] = ((group % 2) * 8 + group // 2) * own_blocks + rows % own_blocks
        copies = [
            pltpu.make_async_copy(found.at[i], link_ref.at[pl.ds(i * LANES, LANES)], link_sem.at[i])
            for i in range(link_lines + lines)
        ]
        for copy in copies:
            copy.start()
        for copy in copies:
            copy.wait()

    def products(u, first, count):
        def some(step, carry):
            for k in range(UNROLL):
                t = first + step * UNROLL + k
                picked = panels[u][link_ref[linked + t]]
                sums[t] = sums[link_ref[t]] + jnp.dot(picked, tiles[t], preferred_element_type=F32)
            return carry

        lax.fori_loop(0, count // UNROLL, some, 0)

    theirs = 1 - y_lo

    def share(u, xx, yl, first=0, count=own_blocks):
        return partial.at[u, pl.ds(row_at(xx, yl) * own_blocks + first, count)]

    def collect(u, xx):
        first = row_at(xx, 0) * own_blocks

        def some(step, carry):
            for k in range(4):
                i = first + step * 4 + k
                partial[u, i] = sums[link_ref[slots + i]].astype(BF16)
            return carry

        lax.fori_loop(0, 2 * own_blocks // 4, some, 0)

    def reduce_copy(u, k):
        if PAIRED[u]:
            src, dst, peer = {
                17: (share(u, x + 2, y_lo, 0, half), got_opp.at[u, 0, pl.ds(0, half)], x_up),
                18: (share(u, x + 2, y_lo, half, half), got_opp.at[u, 1, pl.ds(half, half)], x_down),
                19: (share(u, x + 1, theirs), got_far.at[u, 0, theirs], x_up),
                20: (share(u, x - 1, theirs), got_far.at[u, 1, theirs], x_down),
                21: (share(u, x + 1, y_lo), got_far.at[u, 0, y_lo], x_up),
                22: (share(u, x - 1, y_lo), got_far.at[u, 1, y_lo], x_down),
                23: (share(u, x, theirs), got_pair.at[u], y_pair),
                25: (share(u, x + 2, theirs), got_side.at[u], y_pair),
            }[k]
        else:
            src, dst, peer = {
                17: (share(u, x + 2, 0), got_opp.at[u, 0], x_up),
                18: (share(u, x + 2, 1), got_opp.at[u, 1], x_down),
                19: (share(u, x + 1, 1), got_far.at[u, 0, 1], x_up),
                20: (share(u, x - 1, 0), got_far.at[u, 1, 0], x_down),
                21: (share(u, x + 1, 0), got_far.at[u, 0, 0], x_up),
                22: (share(u, x - 1, 1), got_far.at[u, 1, 1], x_down),
                23: (share(u, x, theirs), got_pair.at[u], y_pair),
            }[k]
        return remote(u, k, src, dst, peer)

    def reduce_first(u):
        collect(u, x + 2)
        for k in (25,) if PAIRED[u] else (17, 18):
            reduce_copy(u, k).start()
        collect(u, x + 1)
        reduce_copy(u, 19).start()
        collect(u, x - 1)
        reduce_copy(u, 20).start()
        collect(u, x)

    def side(u):
        reduce_copy(u, 25).wait_recv()
        add_share(u, x + 2, y_lo, [lambda i: got_side[u, i]])
        reduce_copy(u, 17).start()
        reduce_copy(u, 18).start()

    def add_share(u, xx, yl, terms, start=0, count=own_blocks):
        first = row_at(xx, yl) * own_blocks

        def some(step, carry):
            for k in range(2):
                i = start + step * 2 + k
                total = partial[u, first + i].astype(F32)
                for term in terms:
                    total = total + term(i).astype(F32)
                partial[u, first + i] = total.astype(BF16)
            return carry

        lax.fori_loop(0, count // 2, some, 0)

    def second_a(u):
        reduce_copy(u, 17).wait_recv()
        if PAIRED[u]:
            add_share(u, x + 1, y_lo, [lambda i: got_opp[u, 0, i]], 0, half)
        else:
            add_share(u, x + 1, 0, [lambda i: got_opp[u, 0, i]])
        reduce_copy(u, 21).start()

    def second_b(u):
        reduce_copy(u, 18).wait_recv()
        if PAIRED[u]:
            add_share(u, x - 1, y_lo, [lambda i: got_opp[u, 1, i]], half, half)
        else:
            add_share(u, x - 1, 1, [lambda i: got_opp[u, 1, i]])
        reduce_copy(u, 22).start()

    def reduce_third(u):
        landed(u, 19, got_far.at[u])
        add_share(u, x, theirs, [lambda i: got_far[u, 0, theirs, i], lambda i: got_far[u, 1, theirs, i]])
        reduce_copy(u, 23).start()

    def out_copy(u):
        s, h = u // PARTS, u % PARTS
        return pltpu.make_async_copy(result.at[u], out_ref.at[s, 0, :, pl.ds(h * part, part), :], out_sem.at[u])

    def reduce_last(u):
        reduce_copy(u, 23).wait_recv()
        first = row_at(x, y_lo) * own_blocks

        def some(i, carry):
            total = partial[u, first + i].astype(F32) + got_far[u, 0, y_lo, i].astype(F32)
            total = total + got_far[u, 1, y_lo, i].astype(F32)
            result[u, i] = (total + got_pair[u, i].astype(F32)).astype(BF16)
            return carry

        lax.fori_loop(0, own_blocks, some, 0)
        out_copy(u).start()

    run = slots // 4
    tile_copies = [
        pltpu.make_async_copy(tile_ref.at[pl.ds(q * run, run)], tiles.at[pl.ds(q * run, run)], tile_sem.at[q])
        for q in range(4)
    ]

    loaded = []

    def product_run(q):
        def action(u):
            if q not in loaded:
                loaded.append(q)
                tile_copies[q].wait()
            products(u, q * run, run)

        return action

    actions = {f"p{q}": product_run(q) for q in range(4)}
    for action in (
        own_y, own_z, ring_own_a, ring_own_b, ring_other, half_a, half_b, opposite_own, opposite_other, gathered,
        reduce_first, side, second_a, second_b, reduce_third, reduce_last,
    ):
        actions[action.__name__] = action

    started = False
    for name, u in ORDER:
        if not started and name.startswith("ring"):
            started = True
            link_start()
            for copy in tile_copies:
                copy.start()
            sums[slots] = jnp.zeros(sums.shape[1:], F32)
            link_slots()
        actions[name](u)
    sent = tiles.at[pl.ds(0, 22 * own_blocks * part // pores)]
    for u in range(units):
        remote(u, 0, sent, sent, sibling).wait_send()
        out_copy(u).wait()


def shards(gradients, tile_blocks, tile_rows, tile_cols, tile_counts):
    sets, _, own_blocks, objectives, pores = gradients.shape
    slots = tile_blocks.shape[0]
    row_blocks = own_blocks * lax.axis_size("col")
    column_blocks = own_blocks * lax.axis_size("row")
    units, part = sets * PARTS, objectives // PARTS

    any_space = pl.BlockSpec(memory_space=pl.ANY)
    smem = pl.BlockSpec(memory_space=pltpu.SMEM)
    return pl.pallas_call(
        functools.partial(kernel, sets),
        out_shape=jax.ShapeDtypeStruct(gradients.shape, BF16),
        in_specs=[smem] + [any_space] * 4,
        out_specs=any_space,
        scratch_shapes=[pltpu.VMEM((row_blocks, part, pores), BF16) for _ in range(units)]
        + [
            pltpu.VMEM((slots, pores, pores), BF16),
            pltpu.VMEM((slots + 1, part, pores), F32),
            pltpu.VMEM((units, column_blocks, part, pores), BF16),
            pltpu.VMEM((units, 2, own_blocks, part, pores), BF16),
            pltpu.VMEM((units, 2, 2, own_blocks, part, pores), BF16),
            pltpu.VMEM((units, own_blocks, part, pores), BF16),
            pltpu.VMEM((units, own_blocks, part, pores), BF16),
            pltpu.VMEM((units, own_blocks, part, pores), BF16),
            pltpu.VMEM(((2 * slots + column_blocks) // LANES, LANES), jnp.int32),
            pltpu.VMEM(((2 * slots + column_blocks) // LANES, LANES), jnp.int32),
            pltpu.SMEM((2 * slots + column_blocks,), jnp.int32),
            pltpu.SMEM((slots,), jnp.int32),
            pltpu.SemaphoreType.DMA((units,)),
            pltpu.SemaphoreType.DMA((units, ARRIVALS)),
            pltpu.SemaphoreType.DMA((units,)),
            pltpu.SemaphoreType.DMA((4,)),
            pltpu.SemaphoreType.DMA((units,)),
            pltpu.SemaphoreType.DMA(((2 * slots + column_blocks) // LANES,)),
        ],
        compiler_params=pltpu.CompilerParams(
            collective_id=0, has_side_effects=True, vmem_limit_bytes=60 * 2**20
        ),
        cost_estimate=pl.CostEstimate(
            flops=2 * sets * slots * objectives * pores * pores, bytes_accessed=slots * pores * pores * 2, transcendentals=0
        ),
    )(tile_counts, tile_rows, tile_cols, gradients, tile_blocks)


def solution(mesh):
    in_specs = (
        P(None, "row", "col", None, None),
        P(("row", "col"), None, None),
        P(("row", "col")),
        P(("row", "col")),
        P(("row", "col")),
    )
    out_specs = P(None, "col", "row", None, None)
    return jax.shard_map(shards, mesh=mesh, in_specs=in_specs, out_specs=out_specs, check_vma=False)
```

```python
import functools

import jax
import jax.numpy as jnp
from jax import lax
from jax.experimental import pallas as pl
from jax.experimental.pallas import tpu as pltpu
from jax.sharding import PartitionSpec as P

MESH = pl.DeviceIdType.MESH
PARTS = 2
SIDE = (3, 3, 3, 3, 3, 3)
PAIRED = (False, False, True, True, True, True)
ORDER = (
    ("own_z", 0), ("own_z", 1), ("own_y", 0), ("ring_other", 0), ("own_y", 1), ("ring_own_a", 0), ("own_y", 2),
    ("ring_own_b", 0), ("ring_other", 1), ("opposite_own", 0), ("half_a", 0), ("half_b", 0), ("ring_own_a", 1),
    ("ring_own_b", 1), ("opposite_other", 0), ("own_z", 2), ("half_a", 1), ("opposite_own", 1), ("half_b", 1),
    ("gathered", 0), ("p0", 0), ("ring_other", 2), ("own_y", 4), ("p1", 0), ("p2", 0), ("opposite_other", 1),
    ("ring_own_b", 2), ("ring_own_a", 2), ("reduce_first", 0), ("own_y", 5), ("own_z", 4), ("gathered", 1),
    ("p0", 1), ("p1", 1), ("half_a", 2), ("half_b", 2), ("opposite_own", 2), ("ring_other", 4), ("p2", 1),
    ("reduce_first", 1), ("ring_own_a", 4), ("own_y", 3), ("opposite_other", 2), ("ring_own_b", 4), ("second_a", 0),
    ("second_b", 0), ("gathered", 2), ("own_z", 3), ("p0", 2), ("half_a", 4), ("half_b", 4), ("opposite_own", 4),
    ("p1", 2), ("ring_other", 3), ("p2", 2), ("reduce_first", 2), ("opposite_other", 4), ("ring_own_a", 3),
    ("ring_own_b", 3), ("second_b", 1), ("second_a", 1), ("gathered", 4), ("reduce_third", 0), ("own_z", 5),
    ("p0", 4), ("p1", 4), ("half_b", 3), ("opposite_own", 3), ("half_a", 3), ("side", 2), ("ring_other", 5),
    ("p2", 4), ("reduce_first", 4), ("opposite_other", 3), ("second_a", 2), ("ring_own_a", 5), ("ring_own_b", 5),
    ("second_b", 2), ("gathered", 3), ("p0", 3), ("half_b", 5), ("half_a", 5), ("side", 4), ("opposite_own", 5),
    ("p1", 3), ("p2", 3), ("reduce_first", 3), ("opposite_other", 5), ("second_a", 4), ("reduce_third", 2),
    ("second_b", 4), ("gathered", 5), ("p0", 5), ("p1", 5), ("p2", 5), ("side", 3), ("reduce_first", 5),
    ("second_a", 3), ("reduce_third", 4), ("side", 5), ("reduce_third", 1), ("second_b", 3), ("reduce_last", 0),
    ("second_a", 5), ("second_b", 5), ("reduce_third", 3), ("reduce_third", 5), ("reduce_last", 4),
    ("reduce_last", 2), ("reduce_last", 3), ("reduce_last", 1), ("reduce_last", 5),
)
UNROLL = 64
RUNS = 3
LANES = 128
RECV = (0, 1, 2, 3, 4, 5, 6, 6, 7, 7, 3, 3, 3, 3, 3, 3, 3, 8, 9, 10, 10, 10, 10, 11, 7, 12)
ARRIVALS = 13
BF16 = jnp.bfloat16
F32 = jnp.float32


def kernel(sets, count_ref, rows_ref, cols_ref, grad_ref, tile_ref, out_ref, *scratch):
    units = sets * PARTS
    panels = scratch[:units]
    (
        tiles, sums, partial, got_opp, got_far, got_pair, got_side, result, wanted, found, link_ref, col_ref,
        send_sem, recv_sem, own_sem, tile_sem, out_sem, link_sem,
    ) = scratch[units:]
    slots = tiles.shape[0]
    part, pores = panels[0].shape[1:]
    own_blocks = grad_ref.shape[2]

    row = lax.axis_index("row")
    col = lax.axis_index("col")
    x, y_lo = row // 2, row % 2
    y_hi, z, core = col // 8, (col // 2) % 4, col % 2

    def col_at(yh, zz, cc):
        return (yh * 4 + (zz + 4) % 4) * 2 + cc

    def row_at(xx, yl):
        return ((xx + 4) % 4) * 2 + yl

    z_up, z_down = (row, col_at(y_hi, z + 1, core)), (row, col_at(y_hi, z - 1, core))
    y_far, sibling = (row, col_at(1 - y_hi, z, core)), (row, col_at(y_hi, z, 1 - core))
    x_up, x_down = (row_at(x + 1, y_lo), col), (row_at(x - 1, y_lo), col)
    y_pair = (row_at(x, 1 - y_lo), col)

    barrier = pltpu.get_barrier_semaphore()
    for peer in (z_up, z_down, y_far, sibling, x_up, x_down, y_pair):
        pl.semaphore_signal(barrier, inc=1, device_id=peer, device_id_type=MESH)
    pl.semaphore_wait(barrier, 7)

    def remote(u, k, src, dst, peer):
        return pltpu.make_async_remote_copy(
            src_ref=src,
            dst_ref=dst,
            send_sem=send_sem.at[u],
            recv_sem=recv_sem.at[u, RECV[k]],
            device_id=peer,
            device_id_type=MESH,
        )

    def landed(u, k, region):
        remote(u, k, region, region, sibling).wait_recv()

    def own_slice(u):
        s, h = u // PARTS, u % PARTS
        return grad_ref.at[s, 0, :, pl.ds(h * part, part), :]

    def shard(u, yh, zz, first=0, count=own_blocks):
        return panels[u].at[pl.ds((core * 8 + yh * 4 + (zz + 4) % 4) * own_blocks + first, count)]

    half = own_blocks // 2
    other = 1 - y_hi

    def gather_copy(u, k):
        own = shard(u, y_hi, z)
        if k < 4:
            return remote(u, k, own_slice(u), own, (z_up, z_down, y_far, sibling)[k])
        src, peer = {
            4: (shard(u, other, z), z_up),
            5: (shard(u, other, z), z_down),
            6: (shard(u, y_hi, z - 1, 0, half), z_up),
            7: (shard(u, y_hi, z + 1, half, half), z_down),
            8: (shard(u, other, z - 1, 0, SIDE[u]), z_up),
            9: (shard(u, other, z + 1, own_blocks - SIDE[u], SIDE[u]), z_down),
            24: (shard(u, y_hi, z + 2, SIDE[u], own_blocks - 2 * SIDE[u]), y_far),
            10: (shard(u, other, z), sibling),
            11: (shard(u, y_hi, z - 1), sibling),
            12: (shard(u, y_hi, z + 1), sibling),
            13: (shard(u, other, z - 1), sibling),
            14: (shard(u, other, z + 1), sibling),
            15: (shard(u, y_hi, z + 2), sibling),
            16: (shard(u, other, z + 2), sibling),
        }[k]
        return remote(u, k, src, src, peer)

    def own_copy(u):
        return pltpu.make_async_copy(own_slice(u), shard(u, y_hi, z), own_sem.at[u])

    def send(u, *ks):
        for k in ks:
            gather_copy(u, k).start()

    def arrive(u, *ks):
        for k in ks:
            gather_copy(u, k).wait_recv()

    def own_y(u):
        send(u, 2)

    def own_z(u):
        send(u, 0, 1, 3)
        own_copy(u).start()

    def ring_own_a(u):
        arrive(u, 0)
        send(u, 6, 11)

    def ring_own_b(u):
        arrive(u, 1)
        send(u, 7, 12)

    def ring_other(u):
        arrive(u, 2)
        send(u, 4, 5, 10)

    def half_a(u):
        arrive(u, 4)
        send(u, 8, 13)

    def half_b(u):
        arrive(u, 5)
        send(u, 9, 14)

    def opposite_own(u):
        landed(u, 6, shard(u, y_hi, z + 2))
        if SIDE[u] < half:
            send(u, 24)
        send(u, 15)

    def opposite_other(u):
        landed(u, 8, shard(u, other, z + 2))
        send(u, 16)

    def gathered(u):
        own_copy(u).wait()
        landed(u, 3, panels[u].at[pl.ds((1 - core) * 8 * own_blocks, 8 * own_blocks)])

    lines = slots // LANES
    linked = slots + partial.shape[1]
    link_lines = linked // LANES

    def index_copies():
        copies = [pltpu.make_async_copy(cols_ref, col_ref, link_sem.at[0])]
        for i in range(lines):
            run_i = pl.ds(i * LANES, LANES)
            copies.append(pltpu.make_async_copy(cols_ref.at[run_i], wanted.at[i], link_sem.at[1 + i]))
            copies.append(pltpu.make_async_copy(rows_ref.at[run_i], wanted.at[link_lines + i], link_sem.at[1 + lines + i]))
        return copies

    def link_start():
        wanted[...] = jnp.zeros(wanted.shape, jnp.int32)
        for copy in index_copies():
            copy.start()

    def link_slots():
        for copy in index_copies():
            copy.wait()
        shape = (link_lines, LANES)
        at = lax.broadcasted_iota(jnp.int32, shape, 0) * LANES + lax.broadcasted_iota(jnp.int32, shape, 1)
        target = jnp.where(at < slots, wanted[:link_lines], at - slots)
        limit = jnp.where(at < slots, at, count_ref[0])

        def some(step, latest):
            for k in range(16):
                t = step * 16 + k
                latest = jnp.where((target == col_ref[t]) & (limit > t), t, latest)
            return latest

        found[:link_lines] = lax.fori_loop(0, slots // 16, some, jnp.full(shape, slots, jnp.int32))
        rows = wanted[link_lines:]
        group = rows // own_blocks
        found[link_lines:] = ((group % 2) * 8 + group // 2) * own_blocks + rows % own_blocks
        copies = [
            pltpu.make_async_copy(found.at[i], link_ref.at[pl.ds(i * LANES, LANES)], link_sem.at[i])
            for i in range(link_lines + lines)
        ]
        for copy in copies:
            copy.start()
        for copy in copies:
            copy.wait()

    def products(u, first, count):
        def some(step, carry):
            for k in range(0, UNROLL, 2):
                t = first + step * UNROLL + k
                x0, x1 = panels[u][link_ref[linked + t]], panels[u][link_ref[linked + t + 1]]
                zero = jnp.zeros_like(x0)
                left = jnp.concatenate([jnp.concatenate([x0, zero], 1), jnp.concatenate([zero, x1], 1)], 0)
                both = jnp.dot(left, tiles[pl.ds(t, 2)].reshape(2 * pores, pores), preferred_element_type=F32)
                sums[t] = sums[link_ref[t]] + both[:part]
                sums[t + 1] = sums[link_ref[t + 1]] + both[part:]
            return carry

        lax.fori_loop(0, count // UNROLL, some, 0)

    theirs = 1 - y_lo

    def share(u, xx, yl, first=0, count=own_blocks):
        return partial.at[u, pl.ds(row_at(xx, yl) * own_blocks + first, count)]

    def collect(u, xx):
        first = row_at(xx, 0) * own_blocks

        def some(step, carry):
            for k in range(4):
                i = first + step * 4 + k
                partial[u, i] = sums[link_ref[slots + i]].astype(BF16)
            return carry

        lax.fori_loop(0, 2 * own_blocks // 4, some, 0)

    def reduce_copy(u, k):
        if PAIRED[u]:
            src, dst, peer = {
                17: (share(u, x + 2, y_lo, 0, half), got_opp.at[u, 0, pl.ds(0, half)], x_up),
                18: (share(u, x + 2, y_lo, half, half), got_opp.at[u, 1, pl.ds(half, half)], x_down),
                19: (share(u, x + 1, theirs), got_far.at[u, 0, theirs], x_up),
                20: (share(u, x - 1, theirs), got_far.at[u, 1, theirs], x_down),
                21: (share(u, x + 1, y_lo), got_far.at[u, 0, y_lo], x_up),
                22: (share(u, x - 1, y_lo), got_far.at[u, 1, y_lo], x_down),
                23: (share(u, x, theirs), got_pair.at[u], y_pair),
                25: (share(u, x + 2, theirs), got_side.at[u], y_pair),
            }[k]
        else:
            src, dst, peer = {
                17: (share(u, x + 2, 0), got_opp.at[u, 0], x_up),
                18: (share(u, x + 2, 1), got_opp.at[u, 1], x_down),
                19: (share(u, x + 1, 1), got_far.at[u, 0, 1], x_up),
                20: (share(u, x - 1, 0), got_far.at[u, 1, 0], x_down),
                21: (share(u, x + 1, 0), got_far.at[u, 0, 0], x_up),
                22: (share(u, x - 1, 1), got_far.at[u, 1, 1], x_down),
                23: (share(u, x, theirs), got_pair.at[u], y_pair),
            }[k]
        return remote(u, k, src, dst, peer)

    def reduce_first(u):
        collect(u, x + 2)
        for k in (25,) if PAIRED[u] else (17, 18):
            reduce_copy(u, k).start()
        collect(u, x + 1)
        reduce_copy(u, 19).start()
        collect(u, x - 1)
        reduce_copy(u, 20).start()
        collect(u, x)

    def side(u):
        reduce_copy(u, 25).wait_recv()
        add_share(u, x + 2, y_lo, [lambda i: got_side[u, i]])
        reduce_copy(u, 17).start()
        reduce_copy(u, 18).start()

    def add_share(u, xx, yl, terms, start=0, count=own_blocks):
        first = row_at(xx, yl) * own_blocks

        def some(step, carry):
            for k in range(2):
                i = start + step * 2 + k
                total = partial[u, first + i].astype(F32)
                for term in terms:
                    total = total + term(i).astype(F32)
                partial[u, first + i] = total.astype(BF16)
            return carry

        lax.fori_loop(0, count // 2, some, 0)

    def second_a(u):
        reduce_copy(u, 17).wait_recv()
        if PAIRED[u]:
            add_share(u, x + 1, y_lo, [lambda i: got_opp[u, 0, i]], 0, half)
        else:
            add_share(u, x + 1, 0, [lambda i: got_opp[u, 0, i]])
        reduce_copy(u, 21).start()

    def second_b(u):
        reduce_copy(u, 18).wait_recv()
        if PAIRED[u]:
            add_share(u, x - 1, y_lo, [lambda i: got_opp[u, 1, i]], half, half)
        else:
            add_share(u, x - 1, 1, [lambda i: got_opp[u, 1, i]])
        reduce_copy(u, 22).start()

    def reduce_third(u):
        landed(u, 19, got_far.at[u])
        add_share(u, x, theirs, [lambda i: got_far[u, 0, theirs, i], lambda i: got_far[u, 1, theirs, i]])
        reduce_copy(u, 23).start()

    def out_copy(u):
        s, h = u // PARTS, u % PARTS
        return pltpu.make_async_copy(result.at[u], out_ref.at[s, 0, :, pl.ds(h * part, part), :], out_sem.at[u])

    def reduce_last(u):
        reduce_copy(u, 23).wait_recv()
        first = row_at(x, y_lo) * own_blocks

        def some(i, carry):
            total = partial[u, first + i].astype(F32) + got_far[u, 0, y_lo, i].astype(F32)
            total = total + got_far[u, 1, y_lo, i].astype(F32)
            result[u, i] = (total + got_pair[u, i].astype(F32)).astype(BF16)
            return carry

        lax.fori_loop(0, own_blocks, some, 0)
        out_copy(u).start()

    run = slots // RUNS
    tile_copies = [
        pltpu.make_async_copy(tile_ref.at[pl.ds(q * run, run)], tiles.at[pl.ds(q * run, run)], tile_sem.at[q])
        for q in range(RUNS)
    ]

    loaded = []

    def product_run(q):
        def action(u):
            if q not in loaded:
                loaded.append(q)
                tile_copies[q].wait()
            products(u, q * run, run)

        return action

    actions = {f"p{q}": product_run(q) for q in range(RUNS)}
    for action in (
        own_y, own_z, ring_own_a, ring_own_b, ring_other, half_a, half_b, opposite_own, opposite_other, gathered,
        reduce_first, side, second_a, second_b, reduce_third, reduce_last,
    ):
        actions[action.__name__] = action

    started = False
    for name, u in ORDER:
        if not started and name.startswith("ring"):
            started = True
            link_start()
            for copy in tile_copies:
                copy.start()
            sums[slots] = jnp.zeros(sums.shape[1:], F32)
            link_slots()
        actions[name](u)
    sent = tiles.at[pl.ds(0, 22 * own_blocks * part // pores)]
    for u in range(units):
        remote(u, 0, sent, sent, sibling).wait_send()
        out_copy(u).wait()


def shards(gradients, tile_blocks, tile_rows, tile_cols, tile_counts):
    sets, _, own_blocks, objectives, pores = gradients.shape
    slots = tile_blocks.shape[0]
    row_blocks = own_blocks * lax.axis_size("col")
    column_blocks = own_blocks * lax.axis_size("row")
    units, part = sets * PARTS, objectives // PARTS

    any_space = pl.BlockSpec(memory_space=pl.ANY)
    smem = pl.BlockSpec(memory_space=pltpu.SMEM)
    return pl.pallas_call(
        functools.partial(kernel, sets),
        out_shape=jax.ShapeDtypeStruct(gradients.shape, BF16),
        in_specs=[smem] + [any_space] * 4,
        out_specs=any_space,
        scratch_shapes=[pltpu.VMEM((row_blocks, part, pores), BF16) for _ in range(units)]
        + [
            pltpu.VMEM((slots, pores, pores), BF16),
            pltpu.VMEM((slots + 1, part, pores), F32),
            pltpu.VMEM((units, column_blocks, part, pores), BF16),
            pltpu.VMEM((units, 2, own_blocks, part, pores), BF16),
            pltpu.VMEM((units, 2, 2, own_blocks, part, pores), BF16),
            pltpu.VMEM((units, own_blocks, part, pores), BF16),
            pltpu.VMEM((units, own_blocks, part, pores), BF16),
            pltpu.VMEM((units, own_blocks, part, pores), BF16),
            pltpu.VMEM(((2 * slots + column_blocks) // LANES, LANES), jnp.int32),
            pltpu.VMEM(((2 * slots + column_blocks) // LANES, LANES), jnp.int32),
            pltpu.SMEM((2 * slots + column_blocks,), jnp.int32),
            pltpu.SMEM((slots,), jnp.int32),
            pltpu.SemaphoreType.DMA((units,)),
            pltpu.SemaphoreType.DMA((units, ARRIVALS)),
            pltpu.SemaphoreType.DMA((units,)),
            pltpu.SemaphoreType.DMA((RUNS,)),
            pltpu.SemaphoreType.DMA((units,)),
            pltpu.SemaphoreType.DMA(((2 * slots + column_blocks) // LANES,)),
        ],
        compiler_params=pltpu.CompilerParams(
            collective_id=0, has_side_effects=True, vmem_limit_bytes=60 * 2**20
        ),
        cost_estimate=pl.CostEstimate(
            flops=2 * sets * slots * objectives * pores * pores, bytes_accessed=slots * pores * pores * 2, transcendentals=0
        ),
    )(tile_counts, tile_rows, tile_cols, gradients, tile_blocks)


def solution(mesh):
    in_specs = (
        P(None, "row", "col", None, None),
        P(("row", "col"), None, None),
        P(("row", "col")),
        P(("row", "col")),
        P(("row", "col")),
    )
    out_specs = P(None, "col", "row", None, None)
    return jax.shard_map(shards, mesh=mesh, in_specs=in_specs, out_specs=out_specs, check_vma=False)
```

```python
import functools

import jax
import jax.numpy as jnp
from jax import lax
from jax.experimental import pallas as pl
from jax.experimental.pallas import tpu as pltpu
from jax.sharding import PartitionSpec as P

MESH = pl.DeviceIdType.MESH
PARTS = 2
SIDE = (3, 3, 3, 3, 3, 3)
PAIRED = (False, False, True, True, True, True)
ORDER = (
    ("own_z", 1), ("own_y", 1), ("own_z", 2), ("ring_other", 1), ("own_y", 2), ("ring_own_a", 1), ("ring_own_b", 1),
    ("ring_other", 2), ("ring_own_b", 2), ("ring_own_a", 2), ("own_y", 5), ("opposite_own", 1), ("half_b", 1),
    ("half_a", 1), ("opposite_own", 2), ("own_z", 5), ("opposite_other", 1), ("own_y", 3), ("half_b", 2),
    ("half_a", 2), ("own_y", 4), ("ring_other", 5), ("gathered", 1), ("p0", 1), ("p1", 1), ("opposite_other", 2),
    ("own_y", 0), ("ring_own_a", 5), ("ring_own_b", 5), ("p2", 1), ("own_z", 4), ("reduce_first", 1),
    ("gathered", 2), ("half_b", 5), ("p0", 2), ("half_a", 5), ("ring_other", 4), ("opposite_own", 5), ("p1", 2),
    ("p2", 2), ("reduce_first", 2), ("ring_own_a", 4), ("opposite_other", 5), ("ring_own_b", 4), ("second_b", 1),
    ("second_a", 1), ("own_z", 3), ("gathered", 5), ("p0", 5), ("half_b", 4), ("half_a", 4), ("ring_other", 3),
    ("opposite_own", 4), ("side", 2), ("p1", 5), ("p2", 5), ("reduce_first", 5), ("opposite_other", 4),
    ("ring_own_a", 3), ("ring_own_b", 3), ("second_a", 2), ("second_b", 2), ("gathered", 4), ("own_z", 0), ("p0", 4),
    ("half_b", 3), ("half_a", 3), ("ring_other", 0), ("side", 5), ("opposite_own", 3), ("p1", 4), ("p2", 4),
    ("reduce_first", 4), ("opposite_other", 3), ("second_a", 5), ("second_b", 5), ("ring_own_a", 0),
    ("ring_own_b", 0), ("gathered", 3), ("p0", 3), ("p1", 3), ("half_a", 0), ("opposite_own", 0), ("half_b", 0),
    ("side", 4), ("p2", 3), ("reduce_first", 3), ("opposite_other", 0), ("second_a", 4), ("reduce_third", 5),
    ("second_b", 4), ("reduce_third", 1), ("gathered", 0), ("p0", 0), ("p1", 0), ("side", 3), ("p2", 0),
    ("reduce_first", 0), ("reduce_last", 5), ("reduce_third", 4), ("second_a", 3), ("reduce_last", 1),
    ("reduce_third", 2), ("second_b", 3), ("second_a", 0), ("second_b", 0), ("reduce_third", 3), ("reduce_third", 0),
    ("reduce_last", 3), ("reduce_last", 4), ("reduce_last", 2), ("reduce_last", 0),
)
UNROLL = 64
RUNS = 3
LANES = 128
RECV = (0, 1, 2, 3, 4, 5, 6, 6, 7, 7, 3, 3, 3, 3, 3, 3, 3, 8, 9, 10, 10, 10, 10, 11, 7, 12)
ARRIVALS = 13
BF16 = jnp.bfloat16
F32 = jnp.float32


def kernel(sets, count_ref, rows_ref, cols_ref, grad_ref, tile_ref, out_ref, *scratch):
    units = sets * PARTS
    panels = scratch[:units]
    (
        tiles, sums, partial, got_opp, got_far, got_pair, got_side, result, wanted, found, link_ref, col_ref,
        send_sem, recv_sem, own_sem, tile_sem, out_sem, link_sem,
    ) = scratch[units:]
    slots = tiles.shape[0]
    part, pores = panels[0].shape[1:]
    own_blocks = grad_ref.shape[2]

    row = lax.axis_index("row")
    col = lax.axis_index("col")
    x, y_lo = row // 2, row % 2
    y_hi, z, core = col // 8, (col // 2) % 4, col % 2

    def col_at(yh, zz, cc):
        return (yh * 4 + (zz + 4) % 4) * 2 + cc

    def row_at(xx, yl):
        return ((xx + 4) % 4) * 2 + yl

    z_up, z_down = (row, col_at(y_hi, z + 1, core)), (row, col_at(y_hi, z - 1, core))
    y_far, sibling = (row, col_at(1 - y_hi, z, core)), (row, col_at(y_hi, z, 1 - core))
    x_up, x_down = (row_at(x + 1, y_lo), col), (row_at(x - 1, y_lo), col)
    y_pair = (row_at(x, 1 - y_lo), col)

    barrier = pltpu.get_barrier_semaphore()
    for peer in (z_up, z_down, y_far, sibling, x_up, x_down, y_pair):
        pl.semaphore_signal(barrier, inc=1, device_id=peer, device_id_type=MESH)
    pl.semaphore_wait(barrier, 7)

    def remote(u, k, src, dst, peer):
        return pltpu.make_async_remote_copy(
            src_ref=src,
            dst_ref=dst,
            send_sem=send_sem.at[u],
            recv_sem=recv_sem.at[u, RECV[k]],
            device_id=peer,
            device_id_type=MESH,
        )

    def landed(u, k, region):
        remote(u, k, region, region, sibling).wait_recv()

    def own_slice(u):
        s, h = u // PARTS, u % PARTS
        return grad_ref.at[s, 0, :, pl.ds(h * part, part), :]

    def shard(u, yh, zz, first=0, count=own_blocks):
        return panels[u].at[pl.ds((core * 8 + yh * 4 + (zz + 4) % 4) * own_blocks + first, count)]

    half = own_blocks // 2
    other = 1 - y_hi

    def gather_copy(u, k):
        own = shard(u, y_hi, z)
        if k < 4:
            return remote(u, k, own_slice(u), own, (z_up, z_down, y_far, sibling)[k])
        src, peer = {
            4: (shard(u, other, z), z_up),
            5: (shard(u, other, z), z_down),
            6: (shard(u, y_hi, z - 1, 0, half), z_up),
            7: (shard(u, y_hi, z + 1, half, half), z_down),
            8: (shard(u, other, z - 1, 0, SIDE[u]), z_up),
            9: (shard(u, other, z + 1, own_blocks - SIDE[u], SIDE[u]), z_down),
            24: (shard(u, y_hi, z + 2, SIDE[u], own_blocks - 2 * SIDE[u]), y_far),
            10: (shard(u, other, z), sibling),
            11: (shard(u, y_hi, z - 1), sibling),
            12: (shard(u, y_hi, z + 1), sibling),
            13: (shard(u, other, z - 1), sibling),
            14: (shard(u, other, z + 1), sibling),
            15: (shard(u, y_hi, z + 2), sibling),
            16: (shard(u, other, z + 2), sibling),
        }[k]
        return remote(u, k, src, src, peer)

    def own_copy(u):
        return pltpu.make_async_copy(own_slice(u), shard(u, y_hi, z), own_sem.at[u])

    def send(u, *ks):
        for k in ks:
            gather_copy(u, k).start()

    def arrive(u, *ks):
        for k in ks:
            gather_copy(u, k).wait_recv()

    def own_y(u):
        send(u, 2)

    def own_z(u):
        send(u, 0, 1, 3)
        own_copy(u).start()

    def ring_own_a(u):
        arrive(u, 0)
        send(u, 6, 11)

    def ring_own_b(u):
        arrive(u, 1)
        send(u, 7, 12)

    def ring_other(u):
        arrive(u, 2)
        send(u, 4, 5, 10)

    def half_a(u):
        arrive(u, 4)
        send(u, 8, 13)

    def half_b(u):
        arrive(u, 5)
        send(u, 9, 14)

    def opposite_own(u):
        landed(u, 6, shard(u, y_hi, z + 2))
        if SIDE[u] < half:
            send(u, 24)
        send(u, 15)

    def opposite_other(u):
        landed(u, 8, shard(u, other, z + 2))
        send(u, 16)

    def gathered(u):
        own_copy(u).wait()
        landed(u, 3, panels[u].at[pl.ds((1 - core) * 8 * own_blocks, 8 * own_blocks)])

    lines = slots // LANES
    linked = slots + partial.shape[1]
    link_lines = linked // LANES

    def index_copies():
        copies = [pltpu.make_async_copy(cols_ref, col_ref, link_sem.at[0])]
        for i in range(lines):
            run_i = pl.ds(i * LANES, LANES)
            copies.append(pltpu.make_async_copy(cols_ref.at[run_i], wanted.at[i], link_sem.at[1 + i]))
            copies.append(pltpu.make_async_copy(rows_ref.at[run_i], wanted.at[link_lines + i], link_sem.at[1 + lines + i]))
        return copies

    def link_start():
        wanted[...] = jnp.zeros(wanted.shape, jnp.int32)
        for copy in index_copies():
            copy.start()

    def link_slots():
        for copy in index_copies():
            copy.wait()
        shape = (link_lines, LANES)
        at = lax.broadcasted_iota(jnp.int32, shape, 0) * LANES + lax.broadcasted_iota(jnp.int32, shape, 1)
        target = jnp.where(at < slots, wanted[:link_lines], at - slots)
        limit = jnp.where(at < slots, at, count_ref[0])

        def some(step, latest):
            for k in range(16):
                t = step * 16 + k
                latest = jnp.where((target == col_ref[t]) & (limit > t), t, latest)
            return latest

        found[:link_lines] = lax.fori_loop(0, slots // 16, some, jnp.full(shape, slots, jnp.int32))
        rows = wanted[link_lines:]
        group = rows // own_blocks
        found[link_lines:] = ((group % 2) * 8 + group // 2) * own_blocks + rows % own_blocks
        copies = [
            pltpu.make_async_copy(found.at[i], link_ref.at[pl.ds(i * LANES, LANES)], link_sem.at[i])
            for i in range(link_lines + lines)
        ]
        for copy in copies:
            copy.start()
        for copy in copies:
            copy.wait()

    def products(u, first, count):
        def some(step, carry):
            for k in range(0, UNROLL, 2):
                t = first + step * UNROLL + k
                x0, x1 = panels[u][link_ref[linked + t]], panels[u][link_ref[linked + t + 1]]
                zero = jnp.zeros_like(x0)
                left = jnp.concatenate([jnp.concatenate([x0, zero], 1), jnp.concatenate([zero, x1], 1)], 0)
                both = jnp.dot(left, tiles[pl.ds(t, 2)].reshape(2 * pores, pores), preferred_element_type=F32)
                sums[t] = sums[link_ref[t]] + both[:part]
                sums[t + 1] = sums[link_ref[t + 1]] + both[part:]
            return carry

        lax.fori_loop(0, count // UNROLL, some, 0)

    theirs = 1 - y_lo

    def share(u, xx, yl, first=0, count=own_blocks):
        return partial.at[u, pl.ds(row_at(xx, yl) * own_blocks + first, count)]

    def collect(u, xx):
        first = row_at(xx, 0) * own_blocks

        def some(step, carry):
            for k in range(4):
                i = first + step * 4 + k
                partial[u, i] = sums[link_ref[slots + i]].astype(BF16)
            return carry

        lax.fori_loop(0, 2 * own_blocks // 4, some, 0)

    def reduce_copy(u, k):
        if PAIRED[u]:
            src, dst, peer = {
                17: (share(u, x + 2, y_lo, 0, half), got_opp.at[u, 0, pl.ds(0, half)], x_up),
                18: (share(u, x + 2, y_lo, half, half), got_opp.at[u, 1, pl.ds(half, half)], x_down),
                19: (share(u, x + 1, theirs), got_far.at[u, 0, theirs], x_up),
                20: (share(u, x - 1, theirs), got_far.at[u, 1, theirs], x_down),
                21: (share(u, x + 1, y_lo), got_far.at[u, 0, y_lo], x_up),
                22: (share(u, x - 1, y_lo), got_far.at[u, 1, y_lo], x_down),
                23: (share(u, x, theirs), got_pair.at[u], y_pair),
                25: (share(u, x + 2, theirs), got_side.at[u], y_pair),
            }[k]
        else:
            src, dst, peer = {
                17: (share(u, x + 2, 0), got_opp.at[u, 0], x_up),
                18: (share(u, x + 2, 1), got_opp.at[u, 1], x_down),
                19: (share(u, x + 1, 1), got_far.at[u, 0, 1], x_up),
                20: (share(u, x - 1, 0), got_far.at[u, 1, 0], x_down),
                21: (share(u, x + 1, 0), got_far.at[u, 0, 0], x_up),
                22: (share(u, x - 1, 1), got_far.at[u, 1, 1], x_down),
                23: (share(u, x, theirs), got_pair.at[u], y_pair),
            }[k]
        return remote(u, k, src, dst, peer)

    def reduce_first(u):
        collect(u, x + 2)
        for k in (25,) if PAIRED[u] else (17, 18):
            reduce_copy(u, k).start()
        collect(u, x + 1)
        reduce_copy(u, 19).start()
        collect(u, x - 1)
        reduce_copy(u, 20).start()
        collect(u, x)

    def side(u):
        reduce_copy(u, 25).wait_recv()
        add_share(u, x + 2, y_lo, [lambda i: got_side[u, i]])
        reduce_copy(u, 17).start()
        reduce_copy(u, 18).start()

    def add_share(u, xx, yl, terms, start=0, count=own_blocks):
        first = row_at(xx, yl) * own_blocks

        def some(step, carry):
            for k in range(2):
                i = start + step * 2 + k
                total = partial[u, first + i].astype(F32)
                for term in terms:
                    total = total + term(i).astype(F32)
                partial[u, first + i] = total.astype(BF16)
            return carry

        lax.fori_loop(0, count // 2, some, 0)

    def second_a(u):
        reduce_copy(u, 17).wait_recv()
        if PAIRED[u]:
            add_share(u, x + 1, y_lo, [lambda i: got_opp[u, 0, i]], 0, half)
        else:
            add_share(u, x + 1, 0, [lambda i: got_opp[u, 0, i]])
        reduce_copy(u, 21).start()

    def second_b(u):
        reduce_copy(u, 18).wait_recv()
        if PAIRED[u]:
            add_share(u, x - 1, y_lo, [lambda i: got_opp[u, 1, i]], half, half)
        else:
            add_share(u, x - 1, 1, [lambda i: got_opp[u, 1, i]])
        reduce_copy(u, 22).start()

    def reduce_third(u):
        landed(u, 19, got_far.at[u])
        add_share(u, x, theirs, [lambda i: got_far[u, 0, theirs, i], lambda i: got_far[u, 1, theirs, i]])
        reduce_copy(u, 23).start()

    def out_copy(u):
        s, h = u // PARTS, u % PARTS
        return pltpu.make_async_copy(result.at[u], out_ref.at[s, 0, :, pl.ds(h * part, part), :], out_sem.at[u])

    def reduce_last(u):
        reduce_copy(u, 23).wait_recv()
        first = row_at(x, y_lo) * own_blocks

        def some(i, carry):
            total = partial[u, first + i].astype(F32) + got_far[u, 0, y_lo, i].astype(F32)
            total = total + got_far[u, 1, y_lo, i].astype(F32)
            result[u, i] = (total + got_pair[u, i].astype(F32)).astype(BF16)
            return carry

        lax.fori_loop(0, own_blocks, some, 0)
        out_copy(u).start()

    run = slots // RUNS
    tile_copies = [
        pltpu.make_async_copy(tile_ref.at[pl.ds(q * run, run)], tiles.at[pl.ds(q * run, run)], tile_sem.at[q])
        for q in range(RUNS)
    ]

    loaded = []

    def product_run(q):
        def action(u):
            if q not in loaded:
                loaded.append(q)
                tile_copies[q].wait()
            products(u, q * run, run)

        return action

    actions = {f"p{q}": product_run(q) for q in range(RUNS)}
    for action in (
        own_y, own_z, ring_own_a, ring_own_b, ring_other, half_a, half_b, opposite_own, opposite_other, gathered,
        reduce_first, side, second_a, second_b, reduce_third, reduce_last,
    ):
        actions[action.__name__] = action

    started = False
    for name, u in ORDER:
        if not started and name.startswith("ring"):
            started = True
            link_start()
            for copy in tile_copies:
                copy.start()
            sums[slots] = jnp.zeros(sums.shape[1:], F32)
            link_slots()
        actions[name](u)
    sent = tiles.at[pl.ds(0, 22 * own_blocks * part // pores)]
    for u in range(units):
        remote(u, 0, sent, sent, sibling).wait_send()
        out_copy(u).wait()


def shards(gradients, tile_blocks, tile_rows, tile_cols, tile_counts):
    sets, _, own_blocks, objectives, pores = gradients.shape
    slots = tile_blocks.shape[0]
    row_blocks = own_blocks * lax.axis_size("col")
    column_blocks = own_blocks * lax.axis_size("row")
    units, part = sets * PARTS, objectives // PARTS

    any_space = pl.BlockSpec(memory_space=pl.ANY)
    smem = pl.BlockSpec(memory_space=pltpu.SMEM)
    return pl.pallas_call(
        functools.partial(kernel, sets),
        out_shape=jax.ShapeDtypeStruct(gradients.shape, BF16),
        in_specs=[smem] + [any_space] * 4,
        out_specs=any_space,
        scratch_shapes=[pltpu.VMEM((row_blocks, part, pores), BF16) for _ in range(units)]
        + [
            pltpu.VMEM((slots, pores, pores), BF16),
            pltpu.VMEM((slots + 1, part, pores), F32),
            pltpu.VMEM((units, column_blocks, part, pores), BF16),
            pltpu.VMEM((units, 2, own_blocks, part, pores), BF16),
            pltpu.VMEM((units, 2, 2, own_blocks, part, pores), BF16),
            pltpu.VMEM((units, own_blocks, part, pores), BF16),
            pltpu.VMEM((units, own_blocks, part, pores), BF16),
            pltpu.VMEM((units, own_blocks, part, pores), BF16),
            pltpu.VMEM(((2 * slots + column_blocks) // LANES, LANES), jnp.int32),
            pltpu.VMEM(((2 * slots + column_blocks) // LANES, LANES), jnp.int32),
            pltpu.SMEM((2 * slots + column_blocks,), jnp.int32),
            pltpu.SMEM((slots,), jnp.int32),
            pltpu.SemaphoreType.DMA((units,)),
            pltpu.SemaphoreType.DMA((units, ARRIVALS)),
            pltpu.SemaphoreType.DMA((units,)),
            pltpu.SemaphoreType.DMA((RUNS,)),
            pltpu.SemaphoreType.DMA((units,)),
            pltpu.SemaphoreType.DMA(((2 * slots + column_blocks) // LANES,)),
        ],
        compiler_params=pltpu.CompilerParams(
            collective_id=0, has_side_effects=True, vmem_limit_bytes=60 * 2**20
        ),
        cost_estimate=pl.CostEstimate(
            flops=2 * sets * slots * objectives * pores * pores, bytes_accessed=slots * pores * pores * 2, transcendentals=0
        ),
    )(tile_counts, tile_rows, tile_cols, gradients, tile_blocks)


def solution(mesh):
    in_specs = (
        P(None, "row", "col", None, None),
        P(("row", "col"), None, None),
        P(("row", "col")),
        P(("row", "col")),
        P(("row", "col")),
    )
    out_specs = P(None, "col", "row", None, None)
    return jax.shard_map(shards, mesh=mesh, in_specs=in_specs, out_specs=out_specs, check_vma=False)
```
